32 devices in a mesh: dp: 1, seq: 16 (over z, y, x), head: 2 (over core).
Axes of the slice: x: 2, y: 2, z: 4, core: 2. Of those that a mesh axis runs over, the one named last changes fastest.
Arguments:
- query_rows: bfloat16 [1, 4096, 4096], P('dp', 'seq', 'head'), may hold values from -0.59765625 to 0.59765625
- key_rows: bfloat16 [1, 4096, 4096], P('dp', 'seq', 'head'), may hold values from -0.59765625 to 0.59765625
- value_rows: bfloat16 [1, 4096, 4096], P('dp', 'seq', 'head'), may hold values from -1536 to 1536
- grad_out: bfloat16 [1, 4096, 6144], P('dp', 'seq'), may hold values from -6 to 6
- out_weight: bfloat16 [6144, 4096], P('seq', 'head'), may hold values from -0.09375 to 0.09375
- decay_rates: float32 [32], P('head'), may hold values from 0 to 1, as said below
- doc_blocks: int32 [1, 32], P('dp'), may hold values from 0 to 3, never falling along the last dimension, each value on 1 to 16 neighbouring positions
Outputs:
- grad_query: bfloat16 [1, 4096, 4096], P('dp', 'seq', 'head')
- grad_key: bfloat16 [1, 4096, 4096], P('dp', 'seq', 'head')
- grad_value: bfloat16 [1, 4096, 4096], P('dp', 'seq', 'head')
- grad_weight: float32 [6144, 4096], P('seq', 'head')
The draws below stay inside these ranges and needn't reach their ends.
Inputs may be any that keep to these rules, and one draw needn't show every extreme that they name: `doc_blocks`: in each pack document numbers never fall from block to block; every document covers 1 to 16 blocks, and one covers exactly 16. `decay_rates`: rates are positive.
All inputs are finite; a program needn't handle non-finite values.
Results may differ from the reference program's by a relative error of at most 0.024.
Values may be sent and summed in bfloat16 or wider, within the bound.
A program may use at most 192 MiB of HBM per device.

```python
import math
import jax
import jax.numpy as jnp
import numpy as np
from jax import lax

D = 6144
DH = 128
HEADS = 32
BLOCK = 128
TOK_DEV = 256
PACKS = 1
SEQ_LEN = 4096
BLOCKS = 32
N_SEQ = 16


BIG_LEVEL = 256.0


def draw_decay_rates(key, part):
    slow_key, fast_key, pick_key = jax.random.split(jax.random.fold_in(key, 17), 3)
    length = float(SEQ_LEN)
    span = float(TOK_DEV)
    slow = jnp.exp(jax.random.uniform(slow_key, (HEADS,), jnp.float32, math.log(0.3 / length), math.log(2.0 / length)))
    fast = jnp.exp(jax.random.uniform(fast_key, (HEADS,), jnp.float32, math.log(3.0), math.log(7.0))) / span
    share = 0.5
    chosen = jax.random.uniform(pick_key, (HEADS,), jnp.float32) < share
    return jnp.where(chosen, slow, fast).astype(jnp.float32)


def draw_value_rows(key, part):
    base_key, phase_key = jax.random.split(jax.random.fold_in(key, 29))
    shape = (PACKS, SEQ_LEN, HEADS * DH)
    base = jnp.clip(jax.random.normal(base_key, shape, jnp.float32), -6.0, 6.0)
    phase = jax.random.randint(phase_key, (PACKS, 1), 0, 3).astype(jnp.int32)
    span_number = (jnp.arange(SEQ_LEN).astype(jnp.int32) // TOK_DEV)[None, :]
    level = jnp.where((span_number + phase) % 3 == 0, BIG_LEVEL, 1.0).astype(jnp.float32)
    return (base * level[:, :, None]).astype(jnp.bfloat16)


def spiked(entries, key, source, target, shards_of, factor):
    owner, partner = [(jnp.arange(entries.shape[dim]) // (entries.shape[dim] // shards_of)).reshape([-1 if axis == dim else 1 for axis in range(entries.ndim)]) for dim in (source, target)]
    chosen = jax.random.permutation(key, shards_of)[partner]
    strong = (owner == chosen) | (owner == (partner + shards_of // 2) % shards_of)
    return jnp.where(strong, factor * entries, entries)


def block_scale(own_key, extent, cuts, least, top_value):
    factor_of = 1.0
    for dim, parts in cuts:
        steps = jax.random.uniform(jax.random.fold_in(jax.random.fold_in(own_key, 6), dim), (parts,), jnp.float32, least / len(cuts), top_value / len(cuts))
        factor_of = factor_of * jnp.repeat(jnp.exp(steps), extent[dim] // parts).reshape((-1,) + (1,) * (len(extent) - 1 - dim))
    return factor_of


def length_profile(count, total, reach, lean):
    portions = [(1 << 20) // math.isqrt(grade ** lean) + 1 for grade in range(2, count + 1)]
    rest, given = total - reach - (count - 1), [1] * (count - 1)
    while rest > 0:
        candidates = [i for i in range(count - 1) if given[i] < reach]
        pool, left = sum([portions[i] for i in candidates]), rest
        for i in candidates:
            extra = min(reach - given[i], max(1, left * portions[i] // pool), rest)
            given[i] = given[i] + extra
            rest = rest - extra
    return np.array([reach] + given)


def ragged(key, amount, total, most, slope):
    if amount == 2:
        one = jax.random.randint(key, (), max(1, total - most), min(most, total - 1) + 1)
        return jnp.stack([one, total - one])
    sizes = jnp.asarray(length_profile(amount, total, most, slope), jnp.int32)
    pairs = (amount - 1) // 2
    giver, taker = sizes[1:1 + 2 * pairs:2], sizes[2:2 + 2 * pairs:2]
    room = jnp.minimum(giver - 1, most - taker)
    moved = jax.random.randint(jax.random.fold_in(key, 1), (pairs,), 0, 1 << 20) % (room + 1)
    sizes = sizes.at[1:1 + 2 * pairs:2].set(giver - moved).at[2:2 + 2 * pairs:2].set(taker + moved)
    return sizes[jax.random.permutation(jax.random.fold_in(key, 2), amount)]


def noise(own_key, extent, width, limit, cuts=(), dtype=jnp.bfloat16):
    values = width * jax.random.normal(own_key, extent, jnp.float32)
    if cuts:
        values = values * block_scale(own_key, extent, cuts, -0.22, 0.18)
    return jnp.clip(values, -limit, limit).astype(dtype)


def gaussian_with(key, dims, width, limit, shards, heavy, dtype=jnp.bfloat16):
    values = width * jax.random.normal(key, dims, jnp.float32)
    if shards:
        values = values * block_scale(key, dims, shards, -0.22, 0.18)
    return jnp.clip(spiked(values, jax.random.fold_in(key, 3), *heavy), -limit, limit).astype(dtype)


def setup_inputs(seed: int = 0) -> dict:
    splits = jax.random.split(jax.random.key(seed), 8)
    return {
        "query_rows": noise(splits[0], (PACKS, SEQ_LEN, HEADS * DH), 0.09, 0.59765625, ((1, 16), (2, 2))),
        "key_rows": noise(splits[1], (PACKS, SEQ_LEN, HEADS * DH), 0.09, 0.59765625, ((1, 16), (2, 2))),
        "value_rows": draw_value_rows(jax.random.fold_in(splits[7], 71), 0),
        "grad_out": gaussian_with(splits[3], (PACKS, SEQ_LEN, D), 1.0, 6.0, ((1, 16),), (1, 2, 16, 2.0)),
        "out_weight": noise(splits[4], (D, HEADS * DH), (HEADS * DH) ** -0.5, 0.09375, ((0, 16), (1, 2))),
        "decay_rates": draw_decay_rates(jax.random.fold_in(splits[7], 71), 0),
        "doc_blocks": jax.vmap(lambda own: jnp.searchsorted(jnp.cumsum(ragged(own, max(2, N_SEQ // 4), BLOCKS, BLOCKS // 2, 2)), jnp.arange(BLOCKS), side="right"))(jax.random.split(splits[6], PACKS)).reshape((PACKS, BLOCKS)).astype(jnp.int32),
    }


EPSILON = 1e-05

def rounded(array):
    return lax.optimization_barrier(array.astype(jnp.bfloat16))

def block_docs(doc_row, first_block, block_count, block_len):
    blocks = lax.dynamic_slice_in_dim(doc_row, first_block, block_count)
    return jnp.reshape(jnp.broadcast_to(blocks[:, None], (block_count, block_len)), (block_count * block_len,))

def decay_masks(token_docs, decay_rates, prev_doc, next_doc):
    length = token_docs.shape[0]
    position = jnp.arange(length).astype(jnp.float32)
    rates = decay_rates.astype(jnp.float32)[:, None]
    distance = position[:, None] - position[None, :]
    allowed = jnp.logical_and(distance >= 0, token_docs[:, None] == token_docs[None, :])
    intra = jnp.where(allowed[None], jnp.exp(-rates[:, :, None] * jnp.maximum(distance, 0.0)[None]), 0.0)
    weight_end = jnp.where((token_docs == token_docs[length - 1])[None], jnp.exp(-rates * (length - 1.0 - position)[None]), 0.0)
    weight_start = jnp.where((token_docs == token_docs[0])[None], jnp.exp(-rates * position[None]), 0.0)
    weight_before = jnp.where((token_docs == prev_doc)[None], jnp.exp(-rates * (position + 1.0)[None]), 0.0)
    weight_after = jnp.where((token_docs == next_doc)[None], jnp.exp(-rates * (length - position)[None]), 0.0)
    span_decay = jnp.exp(-decay_rates.astype(jnp.float32) * float(length))
    link_fwd = jnp.where(token_docs[length - 1] == prev_doc, span_decay, 0.0)
    link_rev = jnp.where(token_docs[0] == next_doc, span_decay, 0.0)
    return (intra, weight_end, weight_start, weight_before, weight_after, link_fwd, link_rev)

def local_state(keys_here, values_here, weight_end):
    weighted = rounded(keys_here.astype(jnp.float32) * weight_end.T[:, :, None])
    return jnp.einsum('jhd,jhe->hde', weighted.astype(jnp.float32), values_here.astype(jnp.float32))

def forward_out(queries, keys_here, values_here, intra, weight_before, state_in):
    scores = jnp.einsum('thd,jhd->htj', queries.astype(jnp.float32), keys_here.astype(jnp.float32))
    attention = rounded(scores * intra)
    state_low = rounded(state_in)
    carried = jnp.einsum('thd,hde->the', queries.astype(jnp.float32), state_low.astype(jnp.float32))
    output = jnp.einsum('htj,jhe->the', attention.astype(jnp.float32), values_here.astype(jnp.float32)) + weight_before.T[:, :, None] * carried
    inverse_rms = lax.rsqrt(lax.optimization_barrier(jnp.mean(output * output, axis=-1, keepdims=True)) + EPSILON)
    return (attention, state_low, output * inverse_rms, inverse_rms)

def backward_local(queries, values_here, intra, normal, inverse_rms, grad_normed, weight_start):
    inner = lax.optimization_barrier(jnp.mean(grad_normed * normal, axis=-1, keepdims=True))
    grad_attn = rounded(inverse_rms * (grad_normed - normal * inner))
    grad_scores = rounded(jnp.einsum('the,jhe->htj', grad_attn.astype(jnp.float32), values_here.astype(jnp.float32)) * intra)
    weighted = rounded(queries.astype(jnp.float32) * weight_start.T[:, :, None])
    back_local = jnp.einsum('thd,the->hde', weighted.astype(jnp.float32), grad_attn.astype(jnp.float32))
    return (grad_attn, grad_scores, back_local)

def backward_rest(queries, keys_here, values_here, attention, state_low, grad_attn, grad_scores, weight_before, weight_after, state_back):
    back_low = rounded(state_back).astype(jnp.float32)
    attn_f = grad_attn.astype(jnp.float32)
    score_f = grad_scores.astype(jnp.float32)
    grad_query = jnp.einsum('htj,jhd->thd', score_f, keys_here.astype(jnp.float32)) + weight_before.T[:, :, None] * jnp.einsum('the,hde->thd', attn_f, state_low.astype(jnp.float32))
    grad_key = jnp.einsum('htj,thd->jhd', score_f, queries.astype(jnp.float32)) + weight_after.T[:, :, None] * jnp.einsum('jhe,hde->jhd', values_here.astype(jnp.float32), back_low)
    grad_value = jnp.einsum('htj,the->jhe', attention.astype(jnp.float32), attn_f) + weight_after.T[:, :, None] * jnp.einsum('jhd,hde->jhe', keys_here.astype(jnp.float32), back_low)
    return (grad_query.astype(jnp.bfloat16), grad_key.astype(jnp.bfloat16), grad_value.astype(jnp.bfloat16))

def reference(query_rows, key_rows, value_rows, grad_out, out_weight, decay_rates, doc_blocks):
    block_count = TOK_DEV // BLOCK
    norm_factor = (PACKS * SEQ_LEN) ** (-0.5)
    weight_sum = jnp.zeros((D, HEADS * DH), jnp.float32)
    query_list, key_list, value_list = ([], [], [])
    span_ids = jnp.arange(N_SEQ).astype(jnp.int32)
    for pack_index in range(PACKS):
        queries = query_rows[pack_index].reshape(N_SEQ, TOK_DEV, HEADS, DH)
        keys_all = key_rows[pack_index].reshape(N_SEQ, TOK_DEV, HEADS, DH)
        values_all = value_rows[pack_index].reshape(N_SEQ, TOK_DEV, HEADS, DH)
        doc_row = doc_blocks[pack_index]

        def span_masks(span_index, doc_row=doc_row):
            first_block = (span_index * block_count).astype(jnp.int32)
            token_docs = block_docs(doc_row, first_block, block_count, BLOCK)
            prev_doc = doc_row[jnp.maximum(first_block - 1, 0)]
            next_doc = doc_row[jnp.minimum(first_block + block_count, BLOCKS - 1)]
            return decay_masks(token_docs, decay_rates, prev_doc, next_doc)

        def forward_step(state_in, inputs, span_masks=span_masks):
            span_index, query_span, key_span, value_span = inputs
            mask_set = span_masks(span_index)
            state_local = local_state(key_span, value_span, mask_set[1])
            attention, state_low, normal, inverse_rms = forward_out(query_span, key_span, value_span, mask_set[0], mask_set[3], state_in)
            state_out = mask_set[5][:, None, None] * state_in + state_local
            return (state_out, (state_in, normal.astype(jnp.bfloat16)))
        start_state = jnp.zeros((HEADS, DH, DH), jnp.float32)
        final_state, (states_in, normed) = lax.scan(forward_step, start_state, (span_ids, queries, keys_all, values_all))
        normed_flat = normed.reshape(N_SEQ, TOK_DEV, HEADS * DH)
        grads_pack = grad_out[pack_index].reshape(N_SEQ, TOK_DEV, D)

        def weight_step(running, inputs):
            grad_span, normed_span = inputs
            part = rounded(jnp.dot(grad_span.T, normed_span, preferred_element_type=jnp.float32)).astype(jnp.float32)
            return (running + part, 0)
        weight_sum, ignored = lax.scan(weight_step, weight_sum, (grads_pack, normed_flat))
        grad_normed_all = jnp.dot(grad_out[pack_index], out_weight, preferred_element_type=jnp.float32).reshape(N_SEQ, TOK_DEV, HEADS, DH)

        def backward_step(state_back, inputs, span_masks=span_masks):
            span_index, query_span, key_span, value_span, state_in, grad_normed = inputs
            mask_set = span_masks(span_index)
            attention, state_low, normal, inverse_rms = forward_out(query_span, key_span, value_span, mask_set[0], mask_set[3], state_in)
            grad_attn, grad_scores, back_local = backward_local(query_span, value_span, mask_set[0], normal, inverse_rms, grad_normed, mask_set[2])
            grads = backward_rest(query_span, key_span, value_span, attention, state_low, grad_attn, grad_scores, mask_set[3], mask_set[4], state_back)
            state_next = mask_set[6][:, None, None] * state_back + back_local
            return (state_next, grads)
        final_back, (grad_query, grad_key, grad_value) = lax.scan(backward_step, start_state, (span_ids, queries, keys_all, values_all, states_in, grad_normed_all), reverse=True)
        query_list.append(grad_query.reshape(SEQ_LEN, HEADS * DH))
        key_list.append(grad_key.reshape(SEQ_LEN, HEADS * DH))
        value_list.append(grad_value.reshape(SEQ_LEN, HEADS * DH))
    return (jnp.stack(query_list), jnp.stack(key_list), jnp.stack(value_list), weight_sum * norm_factor)
```

```python
import functools

import jax
import jax.numpy as jnp
from jax import lax
from jax.experimental import pallas as pl
from jax.experimental.pallas import tpu as pltpu
from jax.sharding import Mesh, PartitionSpec as P

BLOCK = 128
EPSILON = 1e-05
SEQ = ("sa", "sb")
F32 = jnp.float32
BF16 = jnp.bfloat16


def mm(a, b, ca, cb):
    return lax.dot_general(a, b, (((ca,), (cb,)), ((), ())), preferred_element_type=F32)


def column(mask_ref, index, rate, offset, sign):
    length = mask_ref.shape[0]
    position = lax.broadcasted_iota(jnp.int32, (length, 1), 0).astype(F32)
    return mask_ref[:, index : index + 1] * jnp.exp(-rate * (offset + sign * position))


def intra_of(allowed_ref, rate):
    shape = allowed_ref.shape
    distance = lax.broadcasted_iota(jnp.int32, shape, 0) - lax.broadcasted_iota(jnp.int32, shape, 1)
    return allowed_ref[...] * jnp.exp(-rate * jnp.maximum(distance, 0).astype(F32))


def attend(rate, allowed_ref, mask_ref, q, k, v, state):
    intra = intra_of(allowed_ref, rate)
    attention = (mm(q, k, 1, 1) * intra).astype(BF16)
    before = column(mask_ref, 2, rate, 1.0, 1.0)
    out = mm(attention, v, 1, 0) + before * mm(q, state, 1, 0)
    inverse_rms = lax.rsqrt(jnp.mean(out * out, axis=-1, keepdims=True) + EPSILON)
    return intra, attention, before, out * inverse_rms, inverse_rms


def local_state_kernel(rates, masks, k_ref, v_ref, out_ref):
    rate = rates[pl.program_id(0)]
    end = column(masks, 0, rate, masks.shape[0] - 1.0, -1.0)
    weighted = (k_ref[...].astype(F32) * end).astype(BF16)
    out_ref[0] = mm(weighted, v_ref[...], 0, 0).astype(BF16)


def forward_kernel(rates, masks, allowed, q, k, v, state, out_ref):
    rate = rates[pl.program_id(0)]
    normal = attend(rate, allowed, masks, q[...], k[...], v[...], state[0])[3]
    out_ref[...] = normal.astype(BF16)


def back_state_kernel(rates, masks, allowed, q, k, v, state, gn, grad_ref, out_ref):
    rate = rates[pl.program_id(0)]
    _, _, _, normal, inverse_rms = attend(
        rate, allowed, masks, q[...], k[...], v[...], state[0]
    )
    grad_normed = gn[...].astype(F32)
    inner = jnp.mean(grad_normed * normal, axis=-1, keepdims=True)
    grad = (inverse_rms * (grad_normed - normal * inner)).astype(BF16)
    grad_ref[...] = grad
    start = column(masks, 1, rate, 0.0, 1.0)
    weighted = (q[...].astype(F32) * start).astype(BF16)
    out_ref[0] = mm(weighted, grad, 0, 0).astype(BF16)


def grads_kernel(rates, masks, allowed, q, k, v, state, back, grad, gq_ref, gk_ref, gv_ref):
    rate = rates[pl.program_id(0)]
    intra = intra_of(allowed, rate)
    attention = (mm(q[...], k[...], 1, 1) * intra).astype(BF16)
    before = column(masks, 2, rate, 1.0, 1.0)
    after = column(masks, 3, rate, masks.shape[0] * 1.0, -1.0)
    scores = (mm(grad[...], v[...], 1, 1) * intra).astype(BF16)
    gq = mm(scores, k[...], 1, 0) + before * mm(grad[...], state[0], 1, 1)
    gk = mm(scores, q[...], 0, 0) + after * mm(v[...], back[0], 1, 1)
    gv = mm(attention, grad[...], 0, 0) + after * mm(k[...], back[0], 1, 0)
    gq_ref[...] = gq.astype(BF16)
    gk_ref[...] = gk.astype(BF16)
    gv_ref[...] = gv.astype(BF16)


def scan_kernel(backward, link, x_ref, out_ref):
    count = x_ref.shape[0]
    state = jnp.zeros(x_ref.shape[1:], F32)
    for step in range(count):
        s = count - 1 - step if backward else step
        out_ref[s] = state.astype(BF16)
        state = link[s] * state + x_ref[s].astype(F32)


def per_head(kernel, heads, tok, dim, fixed, rows, states, extra_rows, outs, flops):
    smem = pl.BlockSpec(memory_space=pltpu.SMEM)
    row_spec = pl.BlockSpec((tok, dim), lambda h: (0, h))
    state_spec = pl.BlockSpec((1, dim, dim), lambda h: (h, 0, 0))
    in_specs = [smem] + [pl.BlockSpec(a.shape, lambda h: (0, 0)) for a in fixed[1:]]
    in_specs += [row_spec] * len(rows) + [state_spec] * len(states) + [row_spec] * len(extra_rows)
    kinds = {
        "row": (row_spec, jax.ShapeDtypeStruct((tok, heads * dim), BF16)),
        "state": (state_spec, jax.ShapeDtypeStruct((heads, dim, dim), BF16)),
    }
    return pl.pallas_call(
        kernel,
        grid=(heads,),
        in_specs=in_specs,
        out_specs=[kinds[o][0] for o in outs],
        out_shape=[kinds[o][1] for o in outs],
        compiler_params=pltpu.CompilerParams(vmem_limit_bytes=24 * 1024 * 1024),
        cost_estimate=pl.CostEstimate(
            flops=flops * heads,
            bytes_accessed=2 * tok * heads * dim * (len(rows) + len(extra_rows) + len(outs)),
            transcendentals=heads * tok * tok,
        ),
    )(*fixed, *rows, *states, *extra_rows)


def local(query_rows, key_rows, value_rows, grad_out, out_weight, decay_rates, doc_blocks):
    tok = query_rows.shape[1]
    heads = decay_rates.shape[0]
    dim = query_rows.shape[2] // heads
    count = lax.axis_size(SEQ)
    span = lax.axis_index(SEQ)
    blocks = tok // BLOCK
    total = doc_blocks.shape[1]
    docs = doc_blocks[0]
    q, k, v = query_rows[0], key_rows[0], value_rows[0]
    rates = decay_rates

    with jax.named_scope("masks"):
        first = span * blocks
        token_docs = jnp.repeat(lax.dynamic_slice_in_dim(docs, first, blocks), BLOCK)
        prev_doc = docs[jnp.maximum(first - 1, 0)]
        next_doc = docs[jnp.minimum(first + blocks, total - 1)]
        position = jnp.arange(tok)
        allowed = (
            (position[:, None] >= position[None, :]) & (token_docs[:, None] == token_docs[None, :])
        ).astype(F32)
        masks = jnp.stack(
            [
                token_docs == token_docs[tok - 1],
                token_docs == token_docs[0],
                token_docs == prev_doc,
                token_docs == next_doc,
            ],
            axis=1,
        ).astype(F32)
        firsts = jnp.arange(count) * blocks
        join_fwd = docs[firsts + blocks - 1] == docs[jnp.maximum(firsts - 1, 0)]
        join_rev = docs[firsts] == docs[jnp.minimum(firsts + blocks, total - 1)]

    fixed = (rates, masks, allowed)
    one = 2 * tok * dim * dim
    pair = 2 * tok * tok * dim

    with jax.named_scope("grad_columns"):
        halves = lax.axis_size("head")
        part_rows = tok // halves
        mine = lax.dynamic_slice_in_dim(grad_out[0], lax.axis_index("head") * part_rows, part_rows)
        groups = lax.axis_size("sa")
        width = mine.shape[1] // groups
        mine = mine.reshape(part_rows, groups, width).transpose(1, 0, 2)
        mine = lax.all_to_all(mine, "sa", 0, 0, tiled=True)
        columns = lax.all_gather(mine, "head", axis=0)
        columns = columns.transpose(1, 0, 2, 3).reshape(groups * tok, width)
    with jax.named_scope("weight_rows"):
        weight = lax.all_gather(out_weight, "sb", axis=0, tiled=True)

    def weights(join, rate):
        return jnp.where(join, jnp.exp(-rate * float(tok)), 0.0)

    def exchanged(states, join, backward):
        rows = heads * dim // count
        assert dim % rows == 0
        parts = lax.all_to_all(states.reshape(count, rows, dim), SEQ, 0, 0, tiled=True)
        done = pl.pallas_call(
            functools.partial(scan_kernel, backward),
            in_specs=[
                pl.BlockSpec(memory_space=pltpu.SMEM),
                pl.BlockSpec(memory_space=pltpu.VMEM),
            ],
            out_specs=pl.BlockSpec(memory_space=pltpu.VMEM),
            out_shape=jax.ShapeDtypeStruct(parts.shape, BF16),
        )(weights(join, rates[span * rows // dim]), parts)
        return lax.all_to_all(done, SEQ, 0, 0, tiled=True).reshape(heads, dim, dim)

    with jax.named_scope("states"):
        (local_states,) = per_head(
            local_state_kernel, heads, tok, dim, fixed[:2], (k, v), (), (), ("state",), one
        )
        state_low = exchanged(local_states, join_fwd, False)
    with jax.named_scope("forward"):
        (normed,) = per_head(
            forward_kernel, heads, tok, dim, fixed, (q, k, v), (state_low,), (), ("row",),
            2 * pair + one,
        )
    with jax.named_scope("grad_normed"):
        partial = jnp.dot(columns, weight, preferred_element_type=F32).astype(BF16)
        grad_normed = lax.psum_scatter(partial, "sa", scatter_dimension=0, tiled=True)
    with jax.named_scope("grad_weight"):
        normed_group = lax.all_gather(normed, "sa", axis=0, tiled=True)
        part = mm(columns, normed_group, 0, 0).astype(BF16)
        weight_part = lax.psum_scatter(part, "sb", scatter_dimension=0, tiled=True)
        norm_factor = (lax.axis_size("dp") * count * tok) ** (-0.5)
        grad_weight = lax.psum(weight_part, "dp").astype(F32) * norm_factor
    with jax.named_scope("back_states"):
        grad_attn, back_local = per_head(
            back_state_kernel, heads, tok, dim, fixed, (q, k, v), (state_low,), (grad_normed,),
            ("row", "state"), 2 * pair + 2 * one,
        )
        back_low = exchanged(back_local, join_rev, True)
    with jax.named_scope("grads"):
        grads = per_head(
            grads_kernel, heads, tok, dim, fixed, (q, k, v), (state_low, back_low), (grad_attn,),
            ("row", "row", "row"), 5 * pair + 3 * one,
        )
    return (grads[0][None], grads[1][None], grads[2][None], grad_weight)


def solution(mesh):
    dp, seq, head = (mesh.shape[name] for name in ("dp", "seq", "head"))
    outer = 4 if seq % 4 == 0 else 1
    fine = Mesh(mesh.devices.reshape(dp, outer, seq // outer, head), ("dp", "sa", "sb", "head"))
    rows = P("dp", SEQ, "head")
    in_specs = (rows, rows, rows, P("dp", SEQ, None), P(SEQ, "head"), P("head"), P("dp", None))
    out_specs = (rows, rows, rows, P(SEQ, "head"))
    return jax.shard_map(local, mesh=fine, in_specs=in_specs, out_specs=out_specs, check_vma=False)
```

```python
import functools

import jax
import jax.numpy as jnp
from jax import lax
from jax.experimental import pallas as pl
from jax.experimental.pallas import tpu as pltpu
from jax.sharding import Mesh, PartitionSpec as P

BLOCK = 128
EPSILON = 1e-05
SEQ = ("sa", "sb")
F32 = jnp.float32
BF16 = jnp.bfloat16


def mm(a, b, ca, cb):
    return lax.dot_general(a, b, (((ca,), (cb,)), ((), ())), preferred_element_type=F32)


def column(mask_ref, index, rate, offset, sign):
    length = mask_ref.shape[0]
    position = lax.broadcasted_iota(jnp.int32, (length, 1), 0).astype(F32)
    return mask_ref[:, index : index + 1] * jnp.exp(-rate * (offset + sign * position))


def intra_of(allowed_ref, rate):
    shape = allowed_ref.shape
    distance = lax.broadcasted_iota(jnp.int32, shape, 0) - lax.broadcasted_iota(jnp.int32, shape, 1)
    return allowed_ref[...] * jnp.exp(-rate * jnp.maximum(distance, 0).astype(F32))


def attend(rate, allowed_ref, mask_ref, q, k, v, state):
    intra = intra_of(allowed_ref, rate)
    attention = (mm(q, k, 1, 1) * intra).astype(BF16)
    before = column(mask_ref, 2, rate, 1.0, 1.0)
    out = mm(attention, v, 1, 0) + before * mm(q, state, 1, 0)
    inverse_rms = lax.rsqrt(jnp.mean(out * out, axis=-1, keepdims=True) + EPSILON)
    return intra, attention, before, out * inverse_rms, inverse_rms


def local_state_kernel(rates, masks, k_ref, v_ref, out_ref):
    rate = rates[pl.program_id(0)]
    end = column(masks, 0, rate, masks.shape[0] - 1.0, -1.0)
    weighted = (k_ref[...].astype(F32) * end).astype(BF16)
    out_ref[0] = mm(weighted, v_ref[...], 0, 0).astype(BF16)


def forward_kernel(rates, masks, allowed, q, k, v, state, out_ref):
    rate = rates[pl.program_id(0)]
    normal = attend(rate, allowed, masks, q[...], k[...], v[...], state[0])[3]
    out_ref[...] = normal.astype(BF16)


def back_state_kernel(rates, masks, allowed, q, k, v, state, gn, grad_ref, out_ref):
    rate = rates[pl.program_id(0)]
    _, _, _, normal, inverse_rms = attend(
        rate, allowed, masks, q[...], k[...], v[...], state[0]
    )
    grad_normed = gn[...].astype(F32)
    inner = jnp.mean(grad_normed * normal, axis=-1, keepdims=True)
    grad = (inverse_rms * (grad_normed - normal * inner)).astype(BF16)
    grad_ref[...] = grad
    start = column(masks, 1, rate, 0.0, 1.0)
    weighted = (q[...].astype(F32) * start).astype(BF16)
    out_ref[0] = mm(weighted, grad, 0, 0).astype(BF16)


def grads_kernel(rates, masks, allowed, q, k, v, state, back, grad, gq_ref, gk_ref, gv_ref):
    rate = rates[pl.program_id(0)]
    intra = intra_of(allowed, rate)
    attention = (mm(q[...], k[...], 1, 1) * intra).astype(BF16)
    before = column(masks, 2, rate, 1.0, 1.0)
    after = column(masks, 3, rate, masks.shape[0] * 1.0, -1.0)
    scores = (mm(grad[...], v[...], 1, 1) * intra).astype(BF16)
    gq = mm(scores, k[...], 1, 0) + before * mm(grad[...], state[0], 1, 1)
    gk = mm(scores, q[...], 0, 0) + after * mm(v[...], back[0], 1, 1)
    gv = mm(attention, grad[...], 0, 0) + after * mm(k[...], back[0], 1, 0)
    gq_ref[...] = gq.astype(BF16)
    gk_ref[...] = gk.astype(BF16)
    gv_ref[...] = gv.astype(BF16)


def scan_kernel(backward, link, x_ref, out_ref):
    count = x_ref.shape[0]
    state = jnp.zeros(x_ref.shape[1:], F32)
    for step in range(count):
        s = count - 1 - step if backward else step
        out_ref[s] = state.astype(BF16)
        state = link[s] * state + x_ref[s].astype(F32)


def per_head(kernel, heads, tok, dim, fixed, rows, states, extra_rows, outs, flops, first=0):
    smem = pl.BlockSpec(memory_space=pltpu.SMEM)
    row_spec = pl.BlockSpec((tok, dim), lambda h: (0, h + first))
    state_spec = pl.BlockSpec((1, dim, dim), lambda h: (h + first, 0, 0))
    row_out = pl.BlockSpec((tok, dim), lambda h: (0, h))
    state_out = pl.BlockSpec((1, dim, dim), lambda h: (h, 0, 0))
    in_specs = [smem] + [pl.BlockSpec(a.shape, lambda h: (0, 0)) for a in fixed[1:]]
    in_specs += [row_spec] * len(rows) + [state_spec] * len(states) + [row_spec] * len(extra_rows)
    kinds = {
        "row": (row_out, jax.ShapeDtypeStruct((tok, heads * dim), BF16)),
        "state": (state_out, jax.ShapeDtypeStruct((heads, dim, dim), BF16)),
    }
    return pl.pallas_call(
        kernel,
        grid=(heads,),
        in_specs=in_specs,
        out_specs=[kinds[o][0] for o in outs],
        out_shape=[kinds[o][1] for o in outs],
        compiler_params=pltpu.CompilerParams(vmem_limit_bytes=24 * 1024 * 1024),
        cost_estimate=pl.CostEstimate(
            flops=flops * heads,
            bytes_accessed=2 * tok * heads * dim * (len(rows) + len(extra_rows) + len(outs)),
            transcendentals=heads * tok * tok,
        ),
    )(*fixed, *rows, *states, *extra_rows)


def swap(piece, axis, step):
    count = lax.axis_size(axis)
    return lax.ppermute(piece, axis, [(i, i ^ step) for i in range(count)])


def pick(pieces, index):
    return lax.dynamic_index_in_dim(jnp.stack(pieces), index, 0, False)


def far_first(count):
    return sorted(range(1, count), key=lambda step: (-bin(step).count("1"), -step))


def local(query_rows, key_rows, value_rows, grad_out, out_weight, decay_rates, doc_blocks):
    tok = query_rows.shape[1]
    heads = decay_rates.shape[0]
    dim = query_rows.shape[2] // heads
    count = lax.axis_size(SEQ)
    span = lax.axis_index(SEQ)
    blocks = tok // BLOCK
    total = doc_blocks.shape[1]
    docs = doc_blocks[0]
    q, k, v = query_rows[0], key_rows[0], value_rows[0]
    rates = decay_rates

    with jax.named_scope("masks"):
        first = span * blocks
        token_docs = jnp.repeat(lax.dynamic_slice_in_dim(docs, first, blocks), BLOCK)
        prev_doc = docs[jnp.maximum(first - 1, 0)]
        next_doc = docs[jnp.minimum(first + blocks, total - 1)]
        position = jnp.arange(tok)
        allowed = (
            (position[:, None] >= position[None, :]) & (token_docs[:, None] == token_docs[None, :])
        ).astype(F32)
        masks = jnp.stack(
            [
                token_docs == token_docs[tok - 1],
                token_docs == token_docs[0],
                token_docs == prev_doc,
                token_docs == next_doc,
            ],
            axis=1,
        ).astype(F32)
        firsts = jnp.arange(count) * blocks
        join_fwd = docs[firsts + blocks - 1] == docs[jnp.maximum(firsts - 1, 0)]
        join_rev = docs[firsts] == docs[jnp.minimum(firsts + blocks, total - 1)]

    fixed = (rates, masks, allowed)
    one = 2 * tok * dim * dim
    pair = 2 * tok * tok * dim

    groups, plane, halves = (lax.axis_size(name) for name in ("sa", "sb", "head"))
    here_a, here_b, half = (lax.axis_index(name) for name in ("sa", "sb", "head"))
    with jax.named_scope("grad_columns"):
        part_rows = tok // halves
        mine = lax.dynamic_slice_in_dim(grad_out[0], half * part_rows, part_rows)
        wide = mine.shape[1] // (groups * plane)
        mine = mine.reshape(part_rows, groups, plane, wide)

        def columns_for(step):
            rows = lax.dynamic_index_in_dim(mine, here_a ^ step, 1, False)
            cuts = [lax.dynamic_index_in_dim(rows, here_b ^ d, 1, False) for d in range(plane)]
            return jnp.concatenate(cuts, axis=1)

        got = {step: swap(columns_for(step), "sa", step) for step in far_first(groups)}
        got[0] = columns_for(0)
    with jax.named_scope("weight_rows"):
        weight = {step: swap(out_weight, "sb", step) for step in far_first(plane)}
        weight[0] = out_weight
    with jax.named_scope("grad_columns"):
        columns = []
        for step in range(groups):
            ways = [got[step]] + [swap(got[step], "head", d) for d in range(1, halves)]
            columns.append(jnp.concatenate([pick(ways, half ^ j) for j in range(halves)], axis=0))

    def weights(join, rate):
        return jnp.where(join, jnp.exp(-rate * float(tok)), 0.0)

    def exchanged(states, join, backward):
        rows = heads * dim // count
        assert dim % rows == 0
        parts = lax.all_to_all(states.reshape(count, rows, dim), SEQ, 0, 0, tiled=True)
        done = pl.pallas_call(
            functools.partial(scan_kernel, backward),
            in_specs=[
                pl.BlockSpec(memory_space=pltpu.SMEM),
                pl.BlockSpec(memory_space=pltpu.VMEM),
            ],
            out_specs=pl.BlockSpec(memory_space=pltpu.VMEM),
            out_shape=jax.ShapeDtypeStruct(parts.shape, BF16),
        )(weights(join, rates[span * rows // dim]), parts)
        return lax.all_to_all(done, SEQ, 0, 0, tiled=True).reshape(heads, dim, dim)

    with jax.named_scope("states"):
        (local_states,) = per_head(
            local_state_kernel, heads, tok, dim, fixed[:2], (k, v), (), (), ("state",), one
        )
        state_low = exchanged(local_states, join_fwd, False)
    cuts = 2 if heads % 2 == 0 else 1
    share = heads // cuts
    with jax.named_scope("forward"):
        normed = []
        for c in range(cuts):
            some = (rates[c * share : (c + 1) * share],) + fixed[1:]
            normed += per_head(
                forward_kernel, share, tok, dim, some, (q, k, v), (state_low,), (), ("row",),
                2 * pair + one, c * share,
            )
    with jax.named_scope("normed_group"):
        group = []
        for piece in normed:
            ways = {step: swap(piece, "sa", step) for step in far_first(groups)}
            group.append(jnp.concatenate([piece] + [ways[d] for d in range(1, groups)], axis=0))
    with jax.named_scope("grad_normed"):
        weight = jnp.concatenate([weight[d] for d in range(plane)], axis=0)
        partial = [
            jnp.dot(part, weight, preferred_element_type=F32).astype(BF16) for part in columns
        ]
        partial = jnp.concatenate([pick(partial, here_a ^ j) for j in range(groups)], axis=0)
        grad_normed = lax.psum_scatter(partial, "sa", scatter_dimension=0, tiled=True)
    with jax.named_scope("grad_weight"):
        columns = jnp.concatenate(columns, axis=0)
        norm_factor = (lax.axis_size("dp") * count * tok) ** (-0.5)
        grad_weight = []
        for piece in group:

            def term(step):
                cut = columns[:, step * wide : (step + 1) * wide]
                return mm(cut, piece, 0, 0).astype(BF16)

            terms = [swap(term(step), "sb", step) for step in far_first(plane)] + [term(0)]
            total_here = sum(t.astype(F32) for t in terms)
            grad_weight.append(lax.psum(total_here, "dp") * norm_factor)
        grad_weight = jnp.concatenate(grad_weight, axis=1)
    with jax.named_scope("back_states"):
        grad_attn, back_local = per_head(
            back_state_kernel, heads, tok, dim, fixed, (q, k, v), (state_low,), (grad_normed,),
            ("row", "state"), 2 * pair + 2 * one,
        )
        back_low = exchanged(back_local, join_rev, True)
    with jax.named_scope("grads"):
        grads = per_head(
            grads_kernel, heads, tok, dim, fixed, (q, k, v), (state_low, back_low), (grad_attn,),
            ("row", "row", "row"), 5 * pair + 3 * one,
        )
    return (grads[0][None], grads[1][None], grads[2][None], grad_weight)


def solution(mesh):
    dp, seq, head = (mesh.shape[name] for name in ("dp", "seq", "head"))
    outer = 4 if seq % 4 == 0 else 1
    fine = Mesh(mesh.devices.reshape(dp, outer, seq // outer, head), ("dp", "sa", "sb", "head"))
    rows = P("dp", SEQ, "head")
    in_specs = (rows, rows, rows, P("dp", SEQ, None), P(SEQ, "head"), P("head"), P("dp", None))
    out_specs = (rows, rows, rows, P(SEQ, "head"))
    return jax.shard_map(local, mesh=fine, in_specs=in_specs, out_specs=out_specs, check_vma=False)
```

```python
import functools

import jax
import jax.numpy as jnp
from jax import lax
from jax.experimental import pallas as pl
from jax.experimental.pallas import tpu as pltpu
from jax.sharding import Mesh, PartitionSpec as P

BLOCK = 128
EPSILON = 1e-05
SEQ = ("sa", "sb")
F32 = jnp.float32
BF16 = jnp.bfloat16


def mm(a, b, ca, cb):
    return lax.dot_general(a, b, (((ca,), (cb,)), ((), ())), preferred_element_type=F32)


def column(mask_ref, index, rate, offset, sign):
    length = mask_ref.shape[0]
    position = lax.broadcasted_iota(jnp.int32, (length, 1), 0).astype(F32)
    return mask_ref[:, index : index + 1] * jnp.exp(-rate * (offset + sign * position))


def intra_of(allowed_ref, rate):
    shape = allowed_ref.shape
    distance = lax.broadcasted_iota(jnp.int32, shape, 0) - lax.broadcasted_iota(jnp.int32, shape, 1)
    return allowed_ref[...] * jnp.exp(-rate * jnp.maximum(distance, 0).astype(F32))


def attend(rate, allowed_ref, mask_ref, q, k, v, state):
    intra = intra_of(allowed_ref, rate)
    attention = (mm(q, k, 1, 1) * intra).astype(BF16)
    before = column(mask_ref, 2, rate, 1.0, 1.0)
    out = mm(attention, v, 1, 0) + before * mm(q, state, 1, 0)
    inverse_rms = lax.rsqrt(jnp.mean(out * out, axis=-1, keepdims=True) + EPSILON)
    return intra, attention, before, out * inverse_rms, inverse_rms


def local_state_kernel(rates, masks, k_ref, v_ref, out_ref):
    rate = rates[pl.program_id(0)]
    end = column(masks, 0, rate, masks.shape[0] - 1.0, -1.0)
    weighted = (k_ref[...].astype(F32) * end).astype(BF16)
    out_ref[0] = mm(weighted, v_ref[...], 0, 0).astype(BF16)


def forward_kernel(rates, masks, allowed, q, k, v, state, out_ref):
    rate = rates[pl.program_id(0)]
    normal = attend(rate, allowed, masks, q[...], k[...], v[...], state[0])[3]
    out_ref[...] = normal.astype(BF16)


def back_state_kernel(rates, masks, allowed, q, k, v, state, gn, grad_ref, out_ref):
    rate = rates[pl.program_id(0)]
    _, _, _, normal, inverse_rms = attend(
        rate, allowed, masks, q[...], k[...], v[...], state[0]
    )
    grad_normed = gn[...].astype(F32)
    inner = jnp.mean(grad_normed * normal, axis=-1, keepdims=True)
    grad = (inverse_rms * (grad_normed - normal * inner)).astype(BF16)
    grad_ref[...] = grad
    start = column(masks, 1, rate, 0.0, 1.0)
    weighted = (q[...].astype(F32) * start).astype(BF16)
    out_ref[0] = mm(weighted, grad, 0, 0).astype(BF16)


def grads_kernel(rates, masks, allowed, q, k, v, state, back, grad, gq_ref, gk_ref, gv_ref):
    rate = rates[pl.program_id(0)]
    intra = intra_of(allowed, rate)
    attention = (mm(q[...], k[...], 1, 1) * intra).astype(BF16)
    before = column(masks, 2, rate, 1.0, 1.0)
    after = column(masks, 3, rate, masks.shape[0] * 1.0, -1.0)
    scores = (mm(grad[...], v[...], 1, 1) * intra).astype(BF16)
    gq = mm(scores, k[...], 1, 0) + before * mm(grad[...], state[0], 1, 1)
    gk = mm(scores, q[...], 0, 0) + after * mm(v[...], back[0], 1, 1)
    gv = mm(attention, grad[...], 0, 0) + after * mm(k[...], back[0], 1, 0)
    gq_ref[...] = gq.astype(BF16)
    gk_ref[...] = gk.astype(BF16)
    gv_ref[...] = gv.astype(BF16)


def scan_kernel(backward, link, x_ref, out_ref):
    count = x_ref.shape[0]
    state = jnp.zeros(x_ref.shape[1:], F32)
    for step in range(count):
        s = count - 1 - step if backward else step
        out_ref[s] = state.astype(BF16)
        state = link[s] * state + x_ref[s].astype(F32)


def per_head(kernel, heads, tok, dim, fixed, rows, states, extra_rows, outs, flops, first=0):
    smem = pl.BlockSpec(memory_space=pltpu.SMEM)
    row_spec = pl.BlockSpec((tok, dim), lambda h: (0, h + first))
    state_spec = pl.BlockSpec((1, dim, dim), lambda h: (h + first, 0, 0))
    row_out = pl.BlockSpec((tok, dim), lambda h: (0, h))
    state_out = pl.BlockSpec((1, dim, dim), lambda h: (h, 0, 0))
    in_specs = [smem] + [pl.BlockSpec(a.shape, lambda h: (0, 0)) for a in fixed[1:]]
    in_specs += [row_spec] * len(rows) + [state_spec] * len(states) + [row_spec] * len(extra_rows)
    kinds = {
        "row": (row_out, jax.ShapeDtypeStruct((tok, heads * dim), BF16)),
        "state": (state_out, jax.ShapeDtypeStruct((heads, dim, dim), BF16)),
    }
    return pl.pallas_call(
        kernel,
        grid=(heads,),
        in_specs=in_specs,
        out_specs=[kinds[o][0] for o in outs],
        out_shape=[kinds[o][1] for o in outs],
        compiler_params=pltpu.CompilerParams(vmem_limit_bytes=24 * 1024 * 1024),
        cost_estimate=pl.CostEstimate(
            flops=flops * heads,
            bytes_accessed=2 * tok * heads * dim * (len(rows) + len(extra_rows) + len(outs)),
            transcendentals=heads * tok * tok,
        ),
    )(*fixed, *rows, *states, *extra_rows)


def swap(piece, axis, step):
    count = lax.axis_size(axis)
    return lax.ppermute(piece, axis, [(i, i ^ step) for i in range(count)])


def pick(pieces, index):
    return lax.dynamic_index_in_dim(jnp.stack(pieces), index, 0, False)


def far_first(count):
    return sorted(range(1, count), key=lambda step: (-bin(step).count("1"), -step))


def local(query_rows, key_rows, value_rows, grad_out, out_weight, decay_rates, doc_blocks):
    tok = query_rows.shape[1]
    heads = decay_rates.shape[0]
    dim = query_rows.shape[2] // heads
    count = lax.axis_size(SEQ)
    span = lax.axis_index(SEQ)
    blocks = tok // BLOCK
    total = doc_blocks.shape[1]
    docs = doc_blocks[0]
    q, k, v = query_rows[0], key_rows[0], value_rows[0]
    rates = decay_rates

    with jax.named_scope("masks"):
        first = span * blocks
        token_docs = jnp.repeat(lax.dynamic_slice_in_dim(docs, first, blocks), BLOCK)
        prev_doc = docs[jnp.maximum(first - 1, 0)]
        next_doc = docs[jnp.minimum(first + blocks, total - 1)]
        position = jnp.arange(tok)
        allowed = (
            (position[:, None] >= position[None, :]) & (token_docs[:, None] == token_docs[None, :])
        ).astype(F32)
        masks = jnp.stack(
            [
                token_docs == token_docs[tok - 1],
                token_docs == token_docs[0],
                token_docs == prev_doc,
                token_docs == next_doc,
            ],
            axis=1,
        ).astype(F32)
        firsts = jnp.arange(count) * blocks
        join_fwd = docs[firsts + blocks - 1] == docs[jnp.maximum(firsts - 1, 0)]
        join_rev = docs[firsts] == docs[jnp.minimum(firsts + blocks, total - 1)]

    fixed = (rates, masks, allowed)
    one = 2 * tok * dim * dim
    pair = 2 * tok * tok * dim

    groups, plane, halves = (lax.axis_size(name) for name in ("sa", "sb", "head"))
    here_a, here_b, half = (lax.axis_index(name) for name in ("sa", "sb", "head"))
    def weights(join, rate):
        return jnp.where(join, jnp.exp(-rate * float(tok)), 0.0)

    def send_parts(states):
        rows = heads * dim // count
        assert dim % rows == 0
        return lax.all_to_all(states.reshape(count, rows, dim), SEQ, 0, 0, tiled=True)

    def scan_parts(parts, join, backward):
        rows = parts.shape[1]
        return pl.pallas_call(
            functools.partial(scan_kernel, backward),
            in_specs=[
                pl.BlockSpec(memory_space=pltpu.SMEM),
                pl.BlockSpec(memory_space=pltpu.VMEM),
            ],
            out_specs=pl.BlockSpec(memory_space=pltpu.VMEM),
            out_shape=jax.ShapeDtypeStruct(parts.shape, BF16),
        )(weights(join, rates[span * rows // dim]), parts)

    def send_back(scanned):
        return lax.all_to_all(scanned, SEQ, 0, 0, tiled=True).reshape(heads, dim, dim)

    with jax.named_scope("weight_rows"):
        weight = {step: swap(out_weight, "sb", step) for step in far_first(plane)}
        weight[0] = out_weight
    with jax.named_scope("states"):
        (local_states,) = per_head(
            local_state_kernel, heads, tok, dim, fixed[:2], (k, v), (), (), ("state",), one
        )
    with jax.named_scope("grad_columns"):
        part_rows = tok // halves
        grads_in, _ = lax.optimization_barrier((grad_out[0], local_states))
        mine = lax.dynamic_slice_in_dim(grads_in, half * part_rows, part_rows)
        wide = mine.shape[1] // (groups * plane)
        mine = mine.reshape(part_rows, groups, plane, wide)

        def columns_for(step):
            rows = lax.dynamic_index_in_dim(mine, here_a ^ step, 1, False)
            cuts = [lax.dynamic_index_in_dim(rows, here_b ^ d, 1, False) for d in range(plane)]
            return jnp.concatenate(cuts, axis=1)

        got = {step: swap(columns_for(step), "sa", step) for step in far_first(groups)}
        got[0] = columns_for(0)
    with jax.named_scope("states"):
        scanned = scan_parts(send_parts(local_states), join_fwd, False)
        _, got = lax.optimization_barrier((scanned, got))
        state_low = send_back(scanned)
    with jax.named_scope("grad_columns"):
        columns = []
        for step in range(groups):
            ways = [got[step]] + [swap(got[step], "head", d) for d in range(1, halves)]
            columns.append(jnp.concatenate([pick(ways, half ^ j) for j in range(halves)], axis=0))

    cuts = 2 if heads % 2 == 0 else 1
    share = heads // cuts
    with jax.named_scope("forward"):
        normed = []
        for c in range(cuts):
            some = (rates[c * share : (c + 1) * share],) + fixed[1:]
            normed += per_head(
                forward_kernel, share, tok, dim, some, (q, k, v), (state_low,), (), ("row",),
                2 * pair + one, c * share,
            )
    with jax.named_scope("normed_group"):
        group = []
        for piece in normed:
            ways = {step: swap(piece, "sa", step) for step in far_first(groups)}
            group.append(jnp.concatenate([piece] + [ways[d] for d in range(1, groups)], axis=0))
    with jax.named_scope("grad_normed"):
        columns, weight, _ = lax.optimization_barrier((columns, weight, normed))
        weight = jnp.concatenate([weight[d] for d in range(plane)], axis=0)
        partial = [
            jnp.dot(part, weight, preferred_element_type=F32).astype(BF16) for part in columns
        ]
        partial = jnp.concatenate([pick(partial, here_a ^ j) for j in range(groups)], axis=0)
        grad_normed = lax.psum_scatter(partial, "sa", scatter_dimension=0, tiled=True)
    with jax.named_scope("grad_weight"):
        columns = jnp.concatenate(columns, axis=0)
        norm_factor = (lax.axis_size("dp") * count * tok) ** (-0.5)
        grad_weight = []
        for piece in group:

            def term(step):
                cut = columns[:, step * wide : (step + 1) * wide]
                return mm(cut, piece, 0, 0).astype(BF16)

            terms = [swap(term(step), "sb", step) for step in far_first(plane)] + [term(0)]
            total_here = sum(t.astype(F32) for t in terms)
            grad_weight.append(lax.psum(total_here, "dp") * norm_factor)
        grad_weight = jnp.concatenate(grad_weight, axis=1)
    with jax.named_scope("back_states"):
        grad_attn, back_local = per_head(
            back_state_kernel, heads, tok, dim, fixed, (q, k, v), (state_low,), (grad_normed,),
            ("row", "state"), 2 * pair + 2 * one,
        )
        back_low = send_back(scan_parts(send_parts(back_local), join_rev, True))
    with jax.named_scope("grads"):
        grads = per_head(
            grads_kernel, heads, tok, dim, fixed, (q, k, v), (state_low, back_low), (grad_attn,),
            ("row", "row", "row"), 5 * pair + 3 * one,
        )
    return (grads[0][None], grads[1][None], grads[2][None], grad_weight)


def solution(mesh):
    dp, seq, head = (mesh.shape[name] for name in ("dp", "seq", "head"))
    outer = 4 if seq % 4 == 0 else 1
    fine = Mesh(mesh.devices.reshape(dp, outer, seq // outer, head), ("dp", "sa", "sb", "head"))
    rows = P("dp", SEQ, "head")
    in_specs = (rows, rows, rows, P("dp", SEQ, None), P(SEQ, "head"), P("head"), P("dp", None))
    out_specs = (rows, rows, rows, P(SEQ, "head"))
    return jax.shard_map(local, mesh=fine, in_specs=in_specs, out_specs=out_specs, check_vma=False)
```

```python
import functools

import jax
import jax.numpy as jnp
from jax import lax
from jax.experimental import pallas as pl
from jax.experimental.pallas import tpu as pltpu
from jax.sharding import Mesh, PartitionSpec as P

BLOCK = 128
EPSILON = 1e-05
SEQ = ("sa", "sb")
F32 = jnp.float32
BF16 = jnp.bfloat16


def mm(a, b, ca, cb):
    return lax.dot_general(a, b, (((ca,), (cb,)), ((), ())), preferred_element_type=F32)


def column(mask_ref, index, rate, offset, sign):
    length = mask_ref.shape[0]
    position = lax.broadcasted_iota(jnp.int32, (length, 1), 0).astype(F32)
    return mask_ref[:, index : index + 1] * jnp.exp(-rate * (offset + sign * position))


def intra_of(allowed_ref, rate):
    shape = allowed_ref.shape
    distance = lax.broadcasted_iota(jnp.int32, shape, 0) - lax.broadcasted_iota(jnp.int32, shape, 1)
    return allowed_ref[...] * jnp.exp(-rate * jnp.maximum(distance, 0).astype(F32))


def attend(rate, allowed_ref, mask_ref, q, k, v, state):
    intra = intra_of(allowed_ref, rate)
    attention = (mm(q, k, 1, 1) * intra).astype(BF16)
    before = column(mask_ref, 2, rate, 1.0, 1.0)
    out = mm(attention, v, 1, 0) + before * mm(q, state, 1, 0)
    inverse_rms = lax.rsqrt(jnp.mean(out * out, axis=-1, keepdims=True) + EPSILON)
    return intra, attention, before, out * inverse_rms, inverse_rms


def local_state_kernel(rates, masks, k_ref, v_ref, out_ref):
    rate = rates[pl.program_id(0)]
    end = column(masks, 0, rate, masks.shape[0] - 1.0, -1.0)
    weighted = (k_ref[...].astype(F32) * end).astype(BF16)
    out_ref[0] = mm(weighted, v_ref[...], 0, 0).astype(BF16)


def forward_kernel(rates, masks, allowed, q, k, v, state, out_ref):
    rate = rates[pl.program_id(0)]
    normal = attend(rate, allowed, masks, q[...], k[...], v[...], state[0])[3]
    out_ref[...] = normal.astype(BF16)


def back_state_kernel(rates, masks, allowed, q, k, v, state, gn, grad_ref, out_ref):
    rate = rates[pl.program_id(0)]
    _, _, _, normal, inverse_rms = attend(
        rate, allowed, masks, q[...], k[...], v[...], state[0]
    )
    grad_normed = gn[...].astype(F32)
    inner = jnp.mean(grad_normed * normal, axis=-1, keepdims=True)
    grad = (inverse_rms * (grad_normed - normal * inner)).astype(BF16)
    grad_ref[...] = grad
    start = column(masks, 1, rate, 0.0, 1.0)
    weighted = (q[...].astype(F32) * start).astype(BF16)
    out_ref[0] = mm(weighted, grad, 0, 0).astype(BF16)


def grads_kernel(rates, masks, allowed, q, k, v, state, back, grad, gq_ref, gk_ref, gv_ref):
    rate = rates[pl.program_id(0)]
    intra = intra_of(allowed, rate)
    attention = (mm(q[...], k[...], 1, 1) * intra).astype(BF16)
    before = column(masks, 2, rate, 1.0, 1.0)
    after = column(masks, 3, rate, masks.shape[0] * 1.0, -1.0)
    scores = (mm(grad[...], v[...], 1, 1) * intra).astype(BF16)
    gq = mm(scores, k[...], 1, 0) + before * mm(grad[...], state[0], 1, 1)
    gk = mm(scores, q[...], 0, 0) + after * mm(v[...], back[0], 1, 1)
    gv = mm(attention, grad[...], 0, 0) + after * mm(k[...], back[0], 1, 0)
    gq_ref[...] = gq.astype(BF16)
    gk_ref[...] = gk.astype(BF16)
    gv_ref[...] = gv.astype(BF16)


def scan_kernel(backward, link, x_ref, out_ref):
    count = x_ref.shape[0]
    state = jnp.zeros(x_ref.shape[1:], F32)
    for step in range(count):
        s = count - 1 - step if backward else step
        out_ref[s] = state.astype(BF16)
        state = link[s] * state + x_ref[s].astype(F32)


def per_head(kernel, heads, tok, dim, fixed, rows, states, extra_rows, outs, flops, first=0):
    smem = pl.BlockSpec(memory_space=pltpu.SMEM)
    row_spec = pl.BlockSpec((tok, dim), lambda h: (0, h + first))
    state_spec = pl.BlockSpec((1, dim, dim), lambda h: (h + first, 0, 0))
    row_out = pl.BlockSpec((tok, dim), lambda h: (0, h))
    state_out = pl.BlockSpec((1, dim, dim), lambda h: (h, 0, 0))
    in_specs = [smem] + [pl.BlockSpec(a.shape, lambda h: (0, 0)) for a in fixed[1:]]
    in_specs += [row_spec] * len(rows) + [state_spec] * len(states) + [row_spec] * len(extra_rows)
    kinds = {
        "row": (row_out, jax.ShapeDtypeStruct((tok, heads * dim), BF16)),
        "state": (state_out, jax.ShapeDtypeStruct((heads, dim, dim), BF16)),
    }
    return pl.pallas_call(
        kernel,
        grid=(heads,),
        in_specs=in_specs,
        out_specs=[kinds[o][0] for o in outs],
        out_shape=[kinds[o][1] for o in outs],
        compiler_params=pltpu.CompilerParams(vmem_limit_bytes=24 * 1024 * 1024),
        cost_estimate=pl.CostEstimate(
            flops=flops * heads,
            bytes_accessed=2 * tok * heads * dim * (len(rows) + len(extra_rows) + len(outs)),
            transcendentals=heads * tok * tok,
        ),
    )(*fixed, *rows, *states, *extra_rows)


def swap(piece, axis, step):
    count = lax.axis_size(axis)
    return lax.ppermute(piece, axis, [(i, i ^ step) for i in range(count)])


def pick(pieces, index):
    return lax.dynamic_index_in_dim(jnp.stack(pieces), index, 0, False)


def far_first(count):
    return sorted(range(1, count), key=lambda step: (-bin(step).count("1"), -step))


def local(query_rows, key_rows, value_rows, grad_out, out_weight, decay_rates, doc_blocks):
    tok = query_rows.shape[1]
    heads = decay_rates.shape[0]
    dim = query_rows.shape[2] // heads
    count = lax.axis_size(SEQ)
    span = lax.axis_index(SEQ)
    blocks = tok // BLOCK
    total = doc_blocks.shape[1]
    docs = doc_blocks[0]
    q, k, v = query_rows[0], key_rows[0], value_rows[0]
    rates = decay_rates

    with jax.named_scope("masks"):
        first = span * blocks
        token_docs = jnp.repeat(lax.dynamic_slice_in_dim(docs, first, blocks), BLOCK)
        prev_doc = docs[jnp.maximum(first - 1, 0)]
        next_doc = docs[jnp.minimum(first + blocks, total - 1)]
        position = jnp.arange(tok)
        allowed = (
            (position[:, None] >= position[None, :]) & (token_docs[:, None] == token_docs[None, :])
        ).astype(F32)
        masks = jnp.stack(
            [
                token_docs == token_docs[tok - 1],
                token_docs == token_docs[0],
                token_docs == prev_doc,
                token_docs == next_doc,
            ],
            axis=1,
        ).astype(F32)
        firsts = jnp.arange(count) * blocks
        join_fwd = docs[firsts + blocks - 1] == docs[jnp.maximum(firsts - 1, 0)]
        join_rev = docs[firsts] == docs[jnp.minimum(firsts + blocks, total - 1)]

    fixed = (rates, masks, allowed)
    one = 2 * tok * dim * dim
    pair = 2 * tok * tok * dim

    groups, plane, halves = (lax.axis_size(name) for name in ("sa", "sb", "head"))
    here_a, here_b, half = (lax.axis_index(name) for name in ("sa", "sb", "head"))
    def weights(join, rate):
        return jnp.where(join, jnp.exp(-rate * float(tok)), 0.0)

    def send_parts(states):
        rows = heads * dim // count
        assert dim % rows == 0
        return lax.all_to_all(states.reshape(count, rows, dim), SEQ, 0, 0, tiled=True)

    def scan_parts(parts, join, backward):
        rows = parts.shape[1]
        return pl.pallas_call(
            functools.partial(scan_kernel, backward),
            in_specs=[
                pl.BlockSpec(memory_space=pltpu.SMEM),
                pl.BlockSpec(memory_space=pltpu.VMEM),
            ],
            out_specs=pl.BlockSpec(memory_space=pltpu.VMEM),
            out_shape=jax.ShapeDtypeStruct(parts.shape, BF16),
        )(weights(join, rates[span * rows // dim]), parts)

    def send_back(scanned):
        return lax.all_to_all(scanned, SEQ, 0, 0, tiled=True).reshape(heads, dim, dim)

    with jax.named_scope("weight_rows"):
        weight = {step: swap(out_weight, "sb", step) for step in far_first(plane)}
        weight[0] = out_weight
    with jax.named_scope("states"):
        (local_states,) = per_head(
            local_state_kernel, heads, tok, dim, fixed[:2], (k, v), (), (), ("state",), one
        )
    with jax.named_scope("grad_columns"):
        part_rows = tok // halves
        grads_in, _ = lax.optimization_barrier((grad_out[0], local_states))
        mine = lax.dynamic_slice_in_dim(grads_in, half * part_rows, part_rows)
        wide = mine.shape[1] // (groups * plane)
        mine = mine.reshape(part_rows, groups, plane, wide)

        def columns_for(step):
            rows = lax.dynamic_index_in_dim(mine, here_a ^ step, 1, False)
            cuts = [lax.dynamic_index_in_dim(rows, here_b ^ d, 1, False) for d in range(plane)]
            return jnp.concatenate(cuts, axis=1)

        got = {step: swap(columns_for(step), "sa", step) for step in far_first(groups)}
        got[0] = columns_for(0)
    with jax.named_scope("states"):
        scanned = scan_parts(send_parts(local_states), join_fwd, False)
        _, got = lax.optimization_barrier((scanned, got))
        state_low = send_back(scanned)
    with jax.named_scope("grad_columns"):
        columns = []
        for step in range(groups):
            ways = [got[step]] + [swap(got[step], "head", d) for d in range(1, halves)]
            columns.append(jnp.concatenate([pick(ways, half ^ j) for j in range(halves)], axis=0))

    cuts = 2 if heads % 2 == 0 else 1
    share = heads // cuts
    with jax.named_scope("forward"):
        normed = []
        for c in range(cuts):
            some = (rates[c * share : (c + 1) * share],) + fixed[1:]
            normed += per_head(
                forward_kernel, share, tok, dim, some, (q, k, v), (state_low,), (), ("row",),
                2 * pair + one, c * share,
            )
    with jax.named_scope("normed_group"):
        group = []
        for piece in normed:
            ways = {step: swap(piece, "sa", step) for step in far_first(groups)}
            group.append(jnp.concatenate([piece] + [ways[d] for d in range(1, groups)], axis=0))
    with jax.named_scope("grad_normed"):
        columns, weight, _ = lax.optimization_barrier((columns, weight, scanned))
        weight = jnp.concatenate([weight[d] for d in range(plane)], axis=0)
        partial = [
            jnp.dot(part, weight, preferred_element_type=F32).astype(BF16) for part in columns
        ]
        partial = jnp.concatenate([pick(partial, here_a ^ j) for j in range(groups)], axis=0)
        grad_normed = lax.psum_scatter(partial, "sa", scatter_dimension=0, tiled=True)
    with jax.named_scope("grad_weight"):
        columns = jnp.concatenate(columns, axis=0)
        norm_factor = (lax.axis_size("dp") * count * tok) ** (-0.5)
        grad_weight = []
        for piece in group:

            def term(step):
                cut = columns[:, step * wide : (step + 1) * wide]
                return mm(cut, piece, 0, 0).astype(BF16)

            terms = [swap(term(step), "sb", step) for step in far_first(plane)] + [term(0)]
            total_here = sum(t.astype(F32) for t in terms)
            grad_weight.append(lax.psum(total_here, "dp") * norm_factor)
        grad_weight = jnp.concatenate(grad_weight, axis=1)
    with jax.named_scope("back_states"):
        grad_attn, back_local = per_head(
            back_state_kernel, heads, tok, dim, fixed, (q, k, v), (state_low,), (grad_normed,),
            ("row", "state"), 2 * pair + 2 * one,
        )
        back_low = send_back(scan_parts(send_parts(back_local), join_rev, True))
    with jax.named_scope("grads"):
        grads = per_head(
            grads_kernel, heads, tok, dim, fixed, (q, k, v), (state_low, back_low), (grad_attn,),
            ("row", "row", "row"), 5 * pair + 3 * one,
        )
    return (grads[0][None], grads[1][None], grads[2][None], grad_weight)


def solution(mesh):
    dp, seq, head = (mesh.shape[name] for name in ("dp", "seq", "head"))
    outer = 4 if seq % 4 == 0 else 1
    fine = Mesh(mesh.devices.reshape(dp, outer, seq // outer, head), ("dp", "sa", "sb", "head"))
    rows = P("dp", SEQ, "head")
    in_specs = (rows, rows, rows, P("dp", SEQ, None), P(SEQ, "head"), P("head"), P("dp", None))
    out_specs = (rows, rows, rows, P(SEQ, "head"))
    return jax.shard_map(local, mesh=fine, in_specs=in_specs, out_specs=out_specs, check_vma=False)
```

```python
import functools

import jax
import jax.numpy as jnp
from jax import lax
from jax.experimental import pallas as pl
from jax.experimental.pallas import tpu as pltpu
from jax.sharding import Mesh, PartitionSpec as P

BLOCK = 128
EPSILON = 1e-05
SEQ = ("sa", "sb")
F32 = jnp.float32
BF16 = jnp.bfloat16


def mm(a, b, ca, cb):
    return lax.dot_general(a, b, (((ca,), (cb,)), ((), ())), preferred_element_type=F32)


def column(mask_ref, index, rate, offset, sign):
    length = mask_ref.shape[0]
    position = lax.broadcasted_iota(jnp.int32, (length, 1), 0).astype(F32)
    return mask_ref[:, index : index + 1] * jnp.exp(-rate * (offset + sign * position))


def intra_of(allowed_ref, rate):
    shape = allowed_ref.shape
    distance = lax.broadcasted_iota(jnp.int32, shape, 0) - lax.broadcasted_iota(jnp.int32, shape, 1)
    return allowed_ref[...] * jnp.exp(-rate * jnp.maximum(distance, 0).astype(F32))


def attend(rate, allowed_ref, mask_ref, q, k, v, state):
    intra = intra_of(allowed_ref, rate)
    attention = (mm(q, k, 1, 1) * intra).astype(BF16)
    before = column(mask_ref, 2, rate, 1.0, 1.0)
    out = mm(attention, v, 1, 0) + before * mm(q, state, 1, 0)
    inverse_rms = lax.rsqrt(jnp.mean(out * out, axis=-1, keepdims=True) + EPSILON)
    return intra, attention, before, out * inverse_rms, inverse_rms


def local_state_kernel(rates, masks, k_ref, v_ref, out_ref):
    rate = rates[pl.program_id(0)]
    end = column(masks, 0, rate, masks.shape[0] - 1.0, -1.0)
    weighted = (k_ref[...].astype(F32) * end).astype(BF16)
    out_ref[0] = mm(weighted, v_ref[...], 0, 0).astype(BF16)


def forward_kernel(rates, masks, allowed, q, k, v, state, out_ref):
    rate = rates[pl.program_id(0)]
    normal = attend(rate, allowed, masks, q[...], k[...], v[...], state[0])[3]
    out_ref[...] = normal.astype(BF16)


def back_state_kernel(rates, masks, allowed, q, k, v, state, gn, grad_ref, out_ref):
    rate = rates[pl.program_id(0)]
    _, _, _, normal, inverse_rms = attend(
        rate, allowed, masks, q[...], k[...], v[...], state[0]
    )
    grad_normed = gn[...].astype(F32)
    inner = jnp.mean(grad_normed * normal, axis=-1, keepdims=True)
    grad = (inverse_rms * (grad_normed - normal * inner)).astype(BF16)
    grad_ref[...] = grad
    start = column(masks, 1, rate, 0.0, 1.0)
    weighted = (q[...].astype(F32) * start).astype(BF16)
    out_ref[0] = mm(weighted, grad, 0, 0).astype(BF16)


def grads_kernel(rates, masks, allowed, q, k, v, state, back, grad, gq_ref, gk_ref, gv_ref):
    rate = rates[pl.program_id(0)]
    intra = intra_of(allowed, rate)
    attention = (mm(q[...], k[...], 1, 1) * intra).astype(BF16)
    before = column(masks, 2, rate, 1.0, 1.0)
    after = column(masks, 3, rate, masks.shape[0] * 1.0, -1.0)
    scores = (mm(grad[...], v[...], 1, 1) * intra).astype(BF16)
    gq = mm(scores, k[...], 1, 0) + before * mm(grad[...], state[0], 1, 1)
    gk = mm(scores, q[...], 0, 0) + after * mm(v[...], back[0], 1, 1)
    gv = mm(attention, grad[...], 0, 0) + after * mm(k[...], back[0], 1, 0)
    gq_ref[...] = gq.astype(BF16)
    gk_ref[...] = gk.astype(BF16)
    gv_ref[...] = gv.astype(BF16)


def scan_kernel(backward, link, x_ref, out_ref):
    count = x_ref.shape[0]
    state = jnp.zeros(x_ref.shape[1:], F32)
    for step in range(count):
        s = count - 1 - step if backward else step
        out_ref[s] = state.astype(BF16)
        state = link[s] * state + x_ref[s].astype(F32)


def per_head(kernel, heads, tok, dim, fixed, rows, states, extra_rows, outs, flops, first=0):
    smem = pl.BlockSpec(memory_space=pltpu.SMEM)
    row_spec = pl.BlockSpec((tok, dim), lambda h: (0, h + first))
    state_spec = pl.BlockSpec((1, dim, dim), lambda h: (h + first, 0, 0))
    row_out = pl.BlockSpec((tok, dim), lambda h: (0, h))
    state_out = pl.BlockSpec((1, dim, dim), lambda h: (h, 0, 0))
    in_specs = [smem] + [pl.BlockSpec(a.shape, lambda h: (0, 0)) for a in fixed[1:]]
    in_specs += [row_spec] * len(rows) + [state_spec] * len(states) + [row_spec] * len(extra_rows)
    kinds = {
        "row": (row_out, jax.ShapeDtypeStruct((tok, heads * dim), BF16)),
        "state": (state_out, jax.ShapeDtypeStruct((heads, dim, dim), BF16)),
    }
    return pl.pallas_call(
        kernel,
        grid=(heads,),
        in_specs=in_specs,
        out_specs=[kinds[o][0] for o in outs],
        out_shape=[kinds[o][1] for o in outs],
        compiler_params=pltpu.CompilerParams(vmem_limit_bytes=24 * 1024 * 1024),
        cost_estimate=pl.CostEstimate(
            flops=flops * heads,
            bytes_accessed=2 * tok * heads * dim * (len(rows) + len(extra_rows) + len(outs)),
            transcendentals=heads * tok * tok,
        ),
    )(*fixed, *rows, *states, *extra_rows)


def swap(piece, axis, step):
    count = lax.axis_size(axis)
    return lax.ppermute(piece, axis, [(i, i ^ step) for i in range(count)])


def pick(pieces, index):
    return lax.dynamic_index_in_dim(jnp.stack(pieces), index, 0, False)


def far_first(count):
    return sorted(range(1, count), key=lambda step: (-bin(step).count("1"), -step))


def local(query_rows, key_rows, value_rows, grad_out, out_weight, decay_rates, doc_blocks):
    tok = query_rows.shape[1]
    heads = decay_rates.shape[0]
    dim = query_rows.shape[2] // heads
    count = lax.axis_size(SEQ)
    span = lax.axis_index(SEQ)
    blocks = tok // BLOCK
    total = doc_blocks.shape[1]
    docs = doc_blocks[0]
    q, k, v = query_rows[0], key_rows[0], value_rows[0]
    rates = decay_rates

    with jax.named_scope("masks"):
        first = span * blocks
        token_docs = jnp.repeat(lax.dynamic_slice_in_dim(docs, first, blocks), BLOCK)
        prev_doc = docs[jnp.maximum(first - 1, 0)]
        next_doc = docs[jnp.minimum(first + blocks, total - 1)]
        position = jnp.arange(tok)
        allowed = (
            (position[:, None] >= position[None, :]) & (token_docs[:, None] == token_docs[None, :])
        ).astype(F32)
        masks = jnp.stack(
            [
                token_docs == token_docs[tok - 1],
                token_docs == token_docs[0],
                token_docs == prev_doc,
                token_docs == next_doc,
            ],
            axis=1,
        ).astype(F32)
        firsts = jnp.arange(count) * blocks
        join_fwd = docs[firsts + blocks - 1] == docs[jnp.maximum(firsts - 1, 0)]
        join_rev = docs[firsts] == docs[jnp.minimum(firsts + blocks, total - 1)]

    fixed = (rates, masks, allowed)
    one = 2 * tok * dim * dim
    pair = 2 * tok * tok * dim

    groups, plane, halves = (lax.axis_size(name) for name in ("sa", "sb", "head"))
    here_a, here_b, half = (lax.axis_index(name) for name in ("sa", "sb", "head"))
    def weights(join, rate):
        return jnp.where(join, jnp.exp(-rate * float(tok)), 0.0)

    def send_parts(states):
        rows = heads * dim // count
        assert dim % rows == 0
        return lax.all_to_all(states.reshape(count, rows, dim), SEQ, 0, 0, tiled=True)

    def scan_parts(parts, join, backward):
        rows = parts.shape[1]
        return pl.pallas_call(
            functools.partial(scan_kernel, backward),
            in_specs=[
                pl.BlockSpec(memory_space=pltpu.SMEM),
                pl.BlockSpec(memory_space=pltpu.VMEM),
            ],
            out_specs=pl.BlockSpec(memory_space=pltpu.VMEM),
            out_shape=jax.ShapeDtypeStruct(parts.shape, BF16),
        )(weights(join, rates[span * rows // dim]), parts)

    def send_back(scanned):
        return lax.all_to_all(scanned, SEQ, 0, 0, tiled=True).reshape(heads, dim, dim)

    with jax.named_scope("weight_rows"):
        weight = {step: swap(out_weight, "sb", step) for step in far_first(plane)}
        weight[0] = out_weight
    with jax.named_scope("states"):
        (local_states,) = per_head(
            local_state_kernel, heads, tok, dim, fixed[:2], (k, v), (), (), ("state",), one
        )
    with jax.named_scope("grad_columns"):
        part_rows = tok // halves
        grads_in, _ = lax.optimization_barrier((grad_out[0], local_states))
        mine = lax.dynamic_slice_in_dim(grads_in, half * part_rows, part_rows)
        wide = mine.shape[1] // (groups * plane)
        mine = mine.reshape(part_rows, groups, plane, wide)

        def columns_for(step):
            rows = lax.dynamic_index_in_dim(mine, here_a ^ step, 1, False)
            cuts = [lax.dynamic_index_in_dim(rows, here_b ^ d, 1, False) for d in range(plane)]
            return jnp.concatenate(cuts, axis=1)

        got = {step: swap(columns_for(step), "sa", step) for step in far_first(groups)}
        got[0] = columns_for(0)
    with jax.named_scope("states"):
        scanned = scan_parts(send_parts(local_states), join_fwd, False)
        _, got = lax.optimization_barrier((scanned, got))
        state_low = send_back(scanned)
    with jax.named_scope("grad_columns"):
        columns = []
        for step in range(groups):
            ways = [got[step]] + [swap(got[step], "head", d) for d in range(1, halves)]
            columns.append(jnp.concatenate([pick(ways, half ^ j) for j in range(halves)], axis=0))

    cuts = 2 if heads % 2 == 0 else 1
    share = heads // cuts
    with jax.named_scope("forward"):
        normed = []
        for c in range(cuts):
            some = (rates[c * share : (c + 1) * share],) + fixed[1:]
            normed += per_head(
                forward_kernel, share, tok, dim, some, (q, k, v), (state_low,), (), ("row",),
                2 * pair + one, c * share,
            )
    with jax.named_scope("normed_group"):
        group = []
        arrived = ()
        for piece in normed:
            piece, _ = lax.optimization_barrier((piece, arrived))
            ways = {step: swap(piece, "sa", step) for step in far_first(groups)}
            arrived = tuple(ways.values())
            group.append(jnp.concatenate([piece] + [ways[d] for d in range(1, groups)], axis=0))
    with jax.named_scope("grad_normed"):
        columns, weight, _ = lax.optimization_barrier((columns, weight, normed))
        weight = jnp.concatenate([weight[d] for d in range(plane)], axis=0)
        partial = [
            jnp.dot(part, weight, preferred_element_type=F32).astype(BF16) for part in columns
        ]
        partial = jnp.concatenate([pick(partial, here_a ^ j) for j in range(groups)], axis=0)
        grad_normed = lax.psum_scatter(partial, "sa", scatter_dimension=0, tiled=True)
    with jax.named_scope("grad_weight"):
        columns = jnp.concatenate(columns, axis=0)
        norm_factor = (lax.axis_size("dp") * count * tok) ** (-0.5)
        grad_weight = []
        for piece in group:

            def term(step):
                cut = columns[:, step * wide : (step + 1) * wide]
                return mm(cut, piece, 0, 0).astype(BF16)

            terms = [swap(term(step), "sb", step) for step in far_first(plane)] + [term(0)]
            total_here = sum(t.astype(F32) for t in terms)
            grad_weight.append(lax.psum(total_here, "dp") * norm_factor)
        grad_weight = jnp.concatenate(grad_weight, axis=1)
    with jax.named_scope("back_states"):
        grad_attn, back_local = per_head(
            back_state_kernel, heads, tok, dim, fixed, (q, k, v), (state_low,), (grad_normed,),
            ("row", "state"), 2 * pair + 2 * one,
        )
        back_low = send_back(scan_parts(send_parts(back_local), join_rev, True))
    with jax.named_scope("grads"):
        grads = per_head(
            grads_kernel, heads, tok, dim, fixed, (q, k, v), (state_low, back_low), (grad_attn,),
            ("row", "row", "row"), 5 * pair + 3 * one,
        )
    return (grads[0][None], grads[1][None], grads[2][None], grad_weight)


def solution(mesh):
    dp, seq, head = (mesh.shape[name] for name in ("dp", "seq", "head"))
    outer = 4 if seq % 4 == 0 else 1
    fine = Mesh(mesh.devices.reshape(dp, outer, seq // outer, head), ("dp", "sa", "sb", "head"))
    rows = P("dp", SEQ, "head")
    in_specs = (rows, rows, rows, P("dp", SEQ, None), P(SEQ, "head"), P("head"), P("dp", None))
    out_specs = (rows, rows, rows, P(SEQ, "head"))
    return jax.shard_map(local, mesh=fine, in_specs=in_specs, out_specs=out_specs, check_vma=False)
```
